32 devices in a mesh: groups: 2 (over x), tenant: 4 (over y, core), tensor: 4 (over z).
Axes of the slice: x: 2, y: 2, z: 4, core: 2. Of those that a mesh axis runs over, the one named last changes fastest.
Arguments:
- tokens: bfloat16 [6144, 8192], P(('groups', 'tenant')), parts along dimension 0, may hold values from -6 to 6
- kv_weight: bfloat16 [8192, 2, 1024], P(None, None, 'tensor'), may hold values from -0.0625 to 0.0625
- cotangent: bfloat16 [6144, 2, 1024], P(('groups', 'tenant'), None, 'tensor'), parts along dimension 0, may hold values from -4 to 4
- a_store: bfloat16 [24, 16, 8192], P('tenant', None, 'tensor'), may hold values from -0.0625 to 0.0625
- b_store: bfloat16 [24, 16, 2, 1024], P('tenant', None, None, 'tensor'), may hold values from -0.625 to 0.625
- tile_tenant: int32 [48], P(('groups', 'tenant')), parts along dimension 0, may hold values from 0 to 23
- tenant_place: int32 [24], replicated, may hold values from 0 to 23, each once
Outputs:
- kv_out: bfloat16 [6144, 2, 1024], P(('groups', 'tenant'), None, 'tensor'), parts along dimension 0
- input_grad: bfloat16 [6144, 8192], P(('groups', 'tenant'), 'tensor'), parts along dimension 0
- a_grad: float32 [48, 16, 8192], P(('groups', 'tenant'), None, 'tensor'), parts along dimension 0
- b_grad: float32 [48, 16, 2, 1024], P(('groups', 'tenant'), None, None, 'tensor'), parts along dimension 0
The draws below stay inside these ranges and needn't reach their ends.
There are 2 independent parts, one for each index of `groups`. The reference program is written for one: setup_inputs(seed, part) draws one part's arguments, and reference() takes and returns one part's arrays. A program takes and returns all parts, laid end to end along the dimension named above; an argument that names none is the same for every part. Nothing has to cross between parts.
Inputs may be any that keep to these rules, and one draw needn't show every extreme that they name: `tile_tenant`: each tile of 128 rows belongs to one tenant. A permutation; the adapters of tenant t are stored at row tenant_place[t], on tenant index tenant_place[t] // 6.
All inputs are finite; a program needn't handle non-finite values.
Results may differ from the reference program's by a relative error of at most 0.014.
Values may be sent and summed in bfloat16 or wider, within the bound.
A program may use at most 128 MiB of HBM per device.

```python
import math
import jax
import jax.numpy as jnp
import numpy as np
from jax import lax

D = 8192
R = 16
TILE = 128
TENANTS = 24
TILES = 24
ROWS = 3072
KVH = 1024
N_TENSOR = 4


def with_ends(array, key, smallest, high):
    longest = array.shape.index(max(array.shape))
    spots = []
    for shift in (0, 1):
        where = [jax.random.randint(jax.random.fold_in(key, axis), (), 0, length) for axis, length in enumerate(array.shape)]
        where[longest] = (where[longest] + shift) % array.shape[longest]
        spots.append(tuple(where))
    return array.at[spots[0]].set(smallest).at[spots[1]].set(high)


def block_levels(rng, shape, cuts, least, top_value):
    loudness = 1.0
    for dim, shards_of in cuts:
        draws = jax.random.uniform(jax.random.fold_in(jax.random.fold_in(rng, 6), dim), (shards_of,), jnp.float32, least / len(cuts), top_value / len(cuts))
        loudness = loudness * jnp.repeat(jnp.exp(draws), shape[dim] // shards_of).reshape((-1,) + (1,) * (len(shape) - 1 - dim))
    return loudness


def rank_bounds(number_of, skew):
    portions = [(1 << 20) // math.isqrt(standing ** skew) + 1 for standing in range(1, number_of + 1)]
    width = 1 + sum(portions) // (1 << 30)
    return np.cumsum(np.array([max(1, weight // width) for weight in portions]))


def skewed_ids(rng, dims, count, slope):
    grid = rank_bounds(count, slope)
    ticket = jax.random.randint(jax.random.fold_in(rng, 1), dims, 0, int(grid[count - 1]))
    rank = jnp.searchsorted(jnp.asarray(grid, jnp.int32), ticket, side="right")
    return jax.random.permutation(jax.random.fold_in(rng, 2), count)[rank].astype(jnp.int32)


def centred(own_key, dims, scale, bound, split=(), kind=jnp.bfloat16):
    array = scale * jax.random.normal(own_key, dims, jnp.float32)
    if split:
        array = array * block_levels(own_key, dims, split, -0.22, 0.18)
    return jnp.clip(array, -bound, bound).astype(kind)


def setup_inputs(seed: int = 0, part: int = 0) -> dict:
    streams_of = jax.random.split(jax.random.key(seed), 8)
    part_splits = jax.random.split(jax.random.fold_in(streams_of[7], part), 8)
    return {
        "tokens": centred(part_splits[0], (ROWS, D), 1.0, 6.0, ((0, 4),)),
        "kv_weight": centred(streams_of[1], (D, 2, KVH), D ** -0.5, 0.0625, ((2, 4),)),
        "cotangent": centred(part_splits[2], (ROWS, 2, KVH), 0.25, 4.0, ((0, 4), (2, 4))),
        "a_store": centred(streams_of[3], (TENANTS, R, D), D ** -0.5, 0.0625, ((0, 4), (2, 4))),
        "b_store": centred(streams_of[4], (TENANTS, R, 2, KVH), 0.04, 0.625, ((0, 4), (3, 4))),
        "tile_tenant": with_ends(skewed_ids(part_splits[5], (TILES,), TENANTS, 2), jax.random.fold_in(part_splits[5], 3), 0, TENANTS - 1).astype(jnp.int32),
        "tenant_place": jax.random.permutation(streams_of[6], TENANTS).astype(jnp.int32),
    }


def reference(tokens, kv_weight, cotangent, a_store, b_store, tile_tenant, tenant_place):
    adapter_scale = 2.0
    storage_row = tenant_place[tile_tenant]
    picked_down_weight = a_store[storage_row]
    picked_up_weight = b_store[storage_row].reshape(TILES, R, 2 * KVH)
    input_tile_list = tokens.reshape(TILES, TILE, D)
    g_flat = cotangent.reshape(ROWS, 2 * KVH)
    gradient_tile_list = g_flat.reshape(TILES, TILE, 2 * KVH)
    w_flat = kv_weight.reshape(D, 2 * KVH)
    rank_projection = jnp.einsum('jtd,jrd->jtr', input_tile_list.astype(jnp.float32), picked_down_weight.astype(jnp.float32)).astype(jnp.bfloat16)
    backward_rank_product = jnp.einsum('jtc,jrc->jtr', gradient_tile_list.astype(jnp.float32), picked_up_weight.astype(jnp.float32)).astype(jnp.bfloat16)
    frozen_output = jnp.dot(tokens, w_flat, preferred_element_type=jnp.float32).reshape(TILES, TILE, 2 * KVH)
    adapter_output = frozen_output + adapter_scale * jnp.einsum('zxg,zgk->zxk', rank_projection.astype(jnp.float32), picked_up_weight.astype(jnp.float32))
    kv_out = adapter_output.reshape(ROWS, 2, KVH).astype(jnp.bfloat16)
    part_cols = KVH // N_TENSOR
    g_split = cotangent.reshape(ROWS, 2, N_TENSOR, part_cols)
    w_split = kv_weight.reshape(D, 2, N_TENSOR, part_cols)
    base_grad = jnp.zeros((ROWS, D), jnp.float32)
    for column_block in range(N_TENSOR):
        g_part = g_split[:, :, column_block, :].reshape(ROWS, 2 * part_cols)
        w_part = w_split[:, :, column_block, :].reshape(D, 2 * part_cols)
        partial_term = jnp.dot(g_part, w_part.T, preferred_element_type=jnp.float32)
        base_grad = base_grad + lax.optimization_barrier(partial_term.astype(jnp.bfloat16)).astype(jnp.float32)
    adapter_delta = adapter_scale * jnp.einsum('xeg,xgl->xel', backward_rank_product.astype(jnp.float32), picked_down_weight.astype(jnp.float32))
    input_grad = (base_grad + adapter_delta.reshape(ROWS, D)).astype(jnp.bfloat16)
    tile_down_weight = adapter_scale * jnp.einsum('kvz,kve->kze', backward_rank_product.astype(jnp.float32), input_tile_list.astype(jnp.float32))
    tile_up_weight = adapter_scale * jnp.einsum('wzy,wzn->wyn', rank_projection.astype(jnp.float32), gradient_tile_list.astype(jnp.float32))
    onehot = (jnp.arange(TENANTS, dtype=jnp.int32)[:, None] == storage_row[None, :]).astype(jnp.float32)
    a_grad = jnp.einsum('pj,jrd->prd', onehot, tile_down_weight, precision=lax.Precision.HIGHEST)
    b_grad = jnp.einsum('pj,jrc->prc', onehot, tile_up_weight, precision=lax.Precision.HIGHEST).reshape(TENANTS, R, 2, KVH)
    return kv_out, input_grad, a_grad, b_grad
```

```python
import jax
import jax.numpy as jnp
from jax import lax
from jax.sharding import PartitionSpec as P

F32 = jnp.float32
BF16 = jnp.bfloat16


def mm(a, b, ca, cb):
    return lax.dot_general(a, b, (((ca,), (cb,)), ((), ())), preferred_element_type=F32)


def local(tokens, kv_weight, cotangent, a_store, b_store, tile_tenant, tenant_place):
    rows, model_width = tokens.shape
    tiles = tile_tenant.shape[0]
    tile_len = rows // tiles
    slots, rank, narrow = a_store.shape
    part_cols = kv_weight.shape[2]
    wide = 2 * part_cols
    tenants = tenant_place.shape[0]
    n_tensor = lax.axis_size("tensor")
    n_tenant = lax.axis_size("tenant")
    n_plane = lax.axis_size("groups") * n_tenant
    my_tensor = lax.axis_index("tensor")
    my_plane = lax.axis_index("groups") * n_tenant + lax.axis_index("tenant")

    b_flat = b_store.reshape(slots, rank, wide)
    a_all = lax.all_gather(a_store, "tenant", axis=0, tiled=True).reshape(-1, narrow)
    b_all = lax.all_gather(b_flat, "tenant", axis=0, tiled=True).reshape(-1, wide)
    stored = a_all.shape[0] // rank

    w_flat = kv_weight.reshape(model_width, wide)
    piece = narrow // n_plane
    w_share = lax.dynamic_index_in_dim(
        w_flat.reshape(n_tensor, n_plane, piece, wide), my_plane, 1, keepdims=False
    )
    w_got = lax.all_to_all(w_share, "tensor", split_axis=0, concat_axis=0, tiled=True)
    w_rows = lax.all_gather(w_got, ("groups", "tenant"), axis=0, tiled=False)
    g_flat = cotangent.reshape(rows, wide)
    g_all = lax.all_gather(g_flat, "tensor", axis=0, tiled=False)

    lookup = tile_tenant[:, None] == jnp.arange(tenants, dtype=jnp.int32)[None, :]
    wanted = jnp.sum(jnp.where(lookup, tenant_place[None, :], 0), axis=1)
    wanted_rows = jnp.repeat(wanted, tile_len)
    mask = wanted_rows[:, None] == (jnp.arange(stored * rank, dtype=jnp.int32) // rank)[None, :]
    fold = (
        (jnp.arange(stored * rank, dtype=jnp.int32) % rank)[:, None]
        == jnp.arange(rank, dtype=jnp.int32)[None, :]
    ).astype(BF16)

    x_cols = lax.dynamic_slice_in_dim(tokens, my_tensor * narrow, narrow, 1)
    shrink_part = jnp.where(mask, mm(x_cols, a_all, 1, 1), 0.0).astype(BF16)
    back_part = jnp.where(mask, mm(g_flat, b_all, 1, 1), 0.0).astype(BF16)
    parts = jnp.concatenate(
        [mm(shrink_part, fold, 1, 0).astype(BF16), mm(back_part, fold, 1, 0).astype(BF16)], axis=1
    )
    sums = lax.psum(parts, "tensor")
    twice = sums + sums
    shrink2 = jnp.where(mask, mm(twice[:, :rank], fold, 1, 1), 0.0).astype(BF16)
    back2 = jnp.where(mask, mm(twice[:, rank:], fold, 1, 1), 0.0).astype(BF16)

    a_part = mm(back2, x_cols, 0, 0).reshape(n_tenant, slots * rank, narrow)
    b_part = mm(shrink2, g_flat, 0, 0).reshape(n_tenant, slots * rank, wide)
    grads = jnp.concatenate([a_part, b_part], axis=2).astype(BF16)
    arrived = lax.all_to_all(grads, "tenant", split_axis=0, concat_axis=0, tiled=True)
    summed = jnp.sum(arrived.astype(F32), axis=0)
    a_grad = summed[:, :narrow].reshape(slots, rank, narrow)
    b_grad = summed[:, narrow:].reshape(slots, rank, 2, part_cols)

    kv_out = (mm(tokens, w_flat, 1, 0) + mm(shrink2, b_all, 1, 0)).astype(BF16)
    kv_out = kv_out.reshape(rows, 2, part_cols)

    total = mm(back2, a_all, 1, 0)
    w_mine = w_rows.transpose(1, 0, 2, 3).reshape(n_tensor, narrow, wide)
    for block in range(n_tensor):
        total = total + mm(g_all[block], w_mine[block], 1, 1)
    input_grad = total.astype(BF16)
    return (kv_out, input_grad, a_grad, b_grad)


def solution(mesh):
    in_specs = (
        P(("groups", "tenant"), None),
        P(None, None, "tensor"),
        P(("groups", "tenant"), None, "tensor"),
        P("tenant", None, "tensor"),
        P("tenant", None, None, "tensor"),
        P(("groups", "tenant")),
        P(),
    )
    out_specs = (
        P(("groups", "tenant"), None, "tensor"),
        P(("groups", "tenant"), "tensor"),
        P(("groups", "tenant"), None, "tensor"),
        P(("groups", "tenant"), None, None, "tensor"),
    )
    return jax.shard_map(local, mesh=mesh, in_specs=in_specs, out_specs=out_specs, check_vma=False)
```

```python
import functools
import jax
import jax.numpy as jnp
from jax import lax
from jax.experimental import pallas as pl
from jax.experimental.pallas import tpu as pltpu
from jax.sharding import PartitionSpec as P

F32 = jnp.float32
BF16 = jnp.bfloat16
MESH = pl.DeviceIdType.MESH


def mm(a, b, ca, cb):
    return lax.dot_general(a, b, (((ca,), (cb,)), ((), ())), preferred_element_type=F32)


def kernel(
    sizes, tokens, weight, g_ref, a_ref, b_ref, want_ref,
    kv_ref, in_ref, ag_ref, bg_ref,
    x_buf, wk_buf, acc, x_cols, w_buf, g_buf, total, rank_out, rank_in, grad_out, grad_in, back_ref,
    x_sem, wk_sem, own_sem, w_send, w_recv, plane_send, sib_send,
    up_send, up_recv, down_send, down_recv, rank_send, rank_recv, grad_send, grad_recv,
):
    n, ng, nt, piece, rank, step = sizes
    rows, width = tokens.shape
    wide = weight.shape[1]
    narrow = x_cols.shape[1]
    stored = a_ref.shape[0]
    owned = stored // nt
    me = lax.axis_index("tensor")
    grp = lax.axis_index("groups")
    ten = lax.axis_index("tenant")
    plane = grp * nt + ten
    side = ten + 1 - 2 * lax.rem(ten, 2)

    def at_tensor(z):
        return (grp, ten, z)

    def line(k):
        return lax.rem(me + k, n)

    def mate(dg, dt):
        return lax.rem(grp + dg, ng), lax.rem(ten + dt, nt)

    barrier = pltpu.get_barrier_semaphore()
    for k in range(1, n):
        pl.semaphore_signal(barrier, inc=1, device_id=at_tensor(line(k)), device_id_type=MESH)
    for dg in range(ng):
        for dt in range(nt):
            if dg or dt:
                g2, t2 = mate(dg, dt)
                pl.semaphore_signal(barrier, inc=1, device_id=(g2, t2, me), device_id_type=MESH)

    def load(c, slot):
        return (
            pltpu.make_async_copy(
                tokens.at[:, pl.ds(pl.multiple_of(c * step, step), step)], x_buf.at[slot], x_sem.at[slot]
            ),
            pltpu.make_async_copy(
                weight.at[pl.ds(pl.multiple_of(c * step, step), step), :], wk_buf.at[slot], wk_sem.at[slot]
            ),
        )

    base = pl.multiple_of(me * narrow, narrow)
    own_x = pltpu.make_async_copy(tokens.at[:, pl.ds(base, narrow)], x_cols, own_sem.at[0])
    own_w = pltpu.make_async_copy(weight.at[pl.ds(base, narrow), :], w_buf.at[me], own_sem.at[1])
    own_x.start()
    for copy in load(0, 0):
        copy.start()
    own_w.start()
    pl.semaphore_wait(barrier, n - 1 + ng * nt - 1)

    def spot(z, p):
        return w_buf.at[z, pl.ds(pl.multiple_of(p * piece, piece), piece), :]

    def remote(src, dst, send, recv, device):
        return pltpu.make_async_remote_copy(
            src_ref=src, dst_ref=dst, send_sem=send, recv_sem=recv, device_id=device, device_id_type=MESH
        )

    w_sends = []
    for k in range(1, n):
        z = line(k)
        start = pl.multiple_of(z * narrow + plane * piece, piece)
        copy = remote(
            weight.at[pl.ds(start, piece), :], spot(me, plane), w_send.at[k], w_recv.at[me, plane], at_tensor(z)
        )
        copy.start()
        w_sends.append(copy)

    def up(s):
        o = jnp.maximum(me - s, 0)
        src = g_ref if s == 0 else g_buf.at[o]
        return (
            jnp.logical_and(me >= s, me < n - 1),
            remote(src, g_buf.at[o], up_send.at[s], up_recv.at[s], at_tensor(jnp.minimum(me + 1, n - 1))),
        )

    def down(s):
        o = jnp.minimum(me + s, n - 1)
        src = g_ref if s == 0 else g_buf.at[o]
        return (
            jnp.logical_and(me + s < n, me > 0),
            remote(src, g_buf.at[o], down_send.at[s], down_recv.at[s], at_tensor(jnp.maximum(me - 1, 0))),
        )

    def push(s):
        for ok, copy in (up(s), down(s)):
            pl.when(ok)(copy.start)

    def arrived(s):
        low, high = me - 1 - s, me + 1 + s
        pl.when(low >= 0)(
            remote(g_ref, g_buf.at[jnp.maximum(low, 0)], up_send.at[s], up_recv.at[s], at_tensor(jnp.maximum(me - 1, 0))).wait_recv
        )
        pl.when(high < n)(
            remote(g_ref, g_buf.at[jnp.minimum(high, n - 1)], down_send.at[s], down_recv.at[s], at_tensor(jnp.minimum(me + 1, n - 1))).wait_recv
        )

    push(0)

    ids = lax.broadcasted_iota(jnp.int32, (stored, rows), 0) // rank
    mask = ids == want_ref[...]
    fold = (
        lax.rem(lax.broadcasted_iota(jnp.int32, (stored, rank), 0), rank)
        == lax.broadcasted_iota(jnp.int32, (stored, rank), 1)
    ).astype(BF16)
    own_x.wait()
    part = jnp.where(mask, mm(a_ref[...], x_cols[...], 1, 1), 0.0).astype(BF16)
    rank_out[:rank, :] = mm(fold, part, 0, 0).astype(BF16)
    part = jnp.where(mask, mm(b_ref[...], g_ref[...], 1, 1), 0.0).astype(BF16)
    rank_out[rank:, :] = mm(fold, part, 0, 0).astype(BF16)
    rank_sends = []
    for k in range(1, n):
        copy = remote(rank_out, rank_in.at[me], rank_send.at[k], rank_recv.at[me], at_tensor(line(k)))
        copy.start()
        rank_sends.append(copy)

    chunks = width // step
    acc[...] = jnp.zeros_like(acc)

    def chunk(c, carry):
        slot = lax.rem(c, 2)

        @pl.when(c + 1 < chunks)
        def _():
            for copy in load(c + 1, 1 - slot):
                copy.start()

        for copy in load(c, slot):
            copy.wait()
        acc[...] += mm(x_buf[slot], wk_buf[slot], 1, 0)
        return carry

    lax.fori_loop(0, chunks, chunk, 0)

    plane_sends, sib_sends = [], []

    def to_side(z, p, i):
        copy = remote(spot(z, p), spot(z, p), sib_send.at[i], w_recv.at[z, p], (grp, side, me))
        copy.start()
        sib_sends.append(copy)

    def wait_piece(z, p):
        remote(spot(z, p), spot(z, p), sib_send.at[0], w_recv.at[z, p], (grp, side, me)).wait_recv()

    others = [(dg, dt) for dg in range(ng) for dt in range(0, nt, 2) if dg or dt]
    for k in range(1, n):
        z = line(k)
        wait_piece(z, plane)
        for dg, dt in others:
            g2, t2 = mate(dg, dt)
            copy = remote(
                spot(z, plane), spot(z, plane), plane_send.at[len(plane_sends)], w_recv.at[z, plane], (g2, t2, me)
            )
            copy.start()
            plane_sends.append(copy)
        to_side(z, plane, len(sib_sends))

    rank_in[me] = rank_out[...]
    for k in range(1, n):
        z = line(k)
        remote(rank_out, rank_in.at[z], rank_send.at[k], rank_recv.at[z], at_tensor(z)).wait_recv()
    whole = rank_in[0].astype(F32)
    for z in range(1, n):
        whole = whole + rank_in[z].astype(F32)
    twice = (whole.astype(BF16).astype(F32) * 2.0).astype(BF16)
    shrink = jnp.where(mask, mm(fold, twice[:rank, :], 1, 0), 0.0).astype(BF16)
    back_ref[...] = jnp.where(mask, mm(fold, twice[rank:, :], 1, 0), 0.0).astype(BF16)

    for p in range(nt):
        part_rows = pl.ds(p * owned, owned)
        grad_out[p, :, :narrow] = mm(back_ref[part_rows, :], x_cols[...], 1, 0).astype(BF16)
    spread = mm(shrink, g_ref[...], 1, 0).astype(BF16)
    for p in range(nt):
        grad_out[p, :, narrow:] = spread[p * owned : (p + 1) * owned, :]
    grad_sends = []
    for dt in range(1, nt):
        t2 = lax.rem(ten + dt, nt)
        copy = remote(grad_out.at[t2], grad_in.at[ten], grad_send.at[dt], grad_recv.at[ten], (grp, t2, me))
        copy.start()
        grad_sends.append(copy)
    kv_ref[...] = (acc[...] + mm(shrink, b_ref[...], 0, 0)).astype(BF16)

    tile = min(narrow, 512)

    def add_block(o, g_block, first):
        def body(c, carry):
            cols = pl.ds(pl.multiple_of(c * tile, tile), tile)
            term = mm(g_block[...], w_buf[o, cols, :], 1, 1)
            if first:
                total[:, cols] = term + mm(back_ref[...], a_ref[:, cols], 0, 0)
            else:
                total[:, cols] += term
            return carry

        lax.fori_loop(0, narrow // tile, body, 0)

    own_w.wait()
    arrived(0)
    if n > 2:
        push(1)
    add_block(me, g_ref, True)
    for k in range(1, n):
        z = line(k)
        for dg, dt in others:
            g2, t2 = mate(dg, dt)
            p = g2 * nt + t2
            wait_piece(z, p)
            to_side(z, p, len(sib_sends))
    for s in range(1, n - 2):
        arrived(s)
        push(s + 1)
    for k in range(1, n):
        z = line(k)
        for dg in range(ng):
            for dt in range(0, nt, 2):
                g2 = lax.rem(grp + dg, ng)
                t2 = lax.rem(side + dt, nt)
                wait_piece(z, g2 * nt + t2)

    def use(s):
        low, high = me - 1 - s, me + 1 + s

        @pl.when(low >= 0)
        def _():
            o = jnp.maximum(low, 0)
            add_block(o, g_buf.at[o], False)

        @pl.when(high < n)
        def _():
            o = jnp.minimum(high, n - 1)
            add_block(o, g_buf.at[o], False)

    for s in range(n - 2):
        use(s)

    grad_in[ten] = grad_out[ten]
    for dt in range(1, nt):
        t2 = lax.rem(ten + dt, nt)
        remote(grad_out.at[t2], grad_in.at[t2], grad_send.at[dt], grad_recv.at[t2], (grp, t2, me)).wait_recv()
    ag = grad_in[0, :, :narrow].astype(F32)
    bg = grad_in[0, :, narrow:].astype(F32)
    for p in range(1, nt):
        ag = ag + grad_in[p, :, :narrow].astype(F32)
        bg = bg + grad_in[p, :, narrow:].astype(F32)
    ag_ref[...] = ag
    bg_ref[...] = bg

    arrived(n - 2)
    use(n - 2)
    in_ref[...] = total[...].astype(BF16)

    for copy in w_sends + plane_sends + sib_sends + rank_sends + grad_sends:
        copy.wait_send()
    for s in range(n - 1):
        for ok, copy in (up(s), down(s)):
            pl.when(ok)(copy.wait_send)


def local(tokens, kv_weight, cotangent, a_store, b_store, tile_tenant, tenant_place):
    rows, model_width = tokens.shape
    tiles = tile_tenant.shape[0]
    tile_len = rows // tiles
    slots, rank, narrow = a_store.shape
    part_cols = kv_weight.shape[2]
    wide = 2 * part_cols
    tenants = tenant_place.shape[0]
    n = lax.axis_size("tensor")
    nt = lax.axis_size("tenant")
    ng = lax.axis_size("groups")
    piece = narrow // (ng * nt)

    a_all = lax.all_gather(a_store, "tenant", axis=0, tiled=True).reshape(-1, narrow)
    b_all = lax.all_gather(b_store.reshape(slots, rank, wide), "tenant", axis=0, tiled=True).reshape(-1, wide)
    stored = a_all.shape[0]
    w_flat = kv_weight.reshape(model_width, wide)
    g_flat = cotangent.reshape(rows, wide)
    lookup = tile_tenant[:, None] == jnp.arange(tenants, dtype=jnp.int32)[None, :]
    wanted = jnp.sum(jnp.where(lookup, tenant_place[None, :], 0), axis=1)
    want_rows = jnp.repeat(wanted, tile_len)[None, :]

    step = 1024 if model_width % 1024 == 0 else model_width // 2
    vmem = pl.BlockSpec(memory_space=pltpu.VMEM)
    hbm = pl.BlockSpec(memory_space=pl.ANY)
    dma = pltpu.SemaphoreType.DMA
    mates = ng * nt // 2
    kv, inp, ag, bg = pl.pallas_call(
        functools.partial(kernel, (n, ng, nt, piece, rank, step)),
        out_shape=(
            jax.ShapeDtypeStruct((rows, wide), BF16),
            jax.ShapeDtypeStruct((rows, narrow), BF16),
            jax.ShapeDtypeStruct((slots * rank, narrow), F32),
            jax.ShapeDtypeStruct((slots * rank, wide), F32),
        ),
        in_specs=[hbm, hbm, vmem, vmem, vmem, vmem],
        out_specs=(vmem, vmem, vmem, vmem),
        scratch_shapes=[
            pltpu.VMEM((2, rows, step), BF16),
            pltpu.VMEM((2, step, wide), BF16),
            pltpu.VMEM((rows, wide), F32),
            pltpu.VMEM((rows, narrow), BF16),
            pltpu.VMEM((n, narrow, wide), BF16),
            pltpu.VMEM((n, rows, wide), BF16),
            pltpu.VMEM((rows, narrow), F32),
            pltpu.VMEM((2 * rank, rows), BF16),
            pltpu.VMEM((n, 2 * rank, rows), BF16),
            pltpu.VMEM((nt, slots * rank, narrow + wide), BF16),
            pltpu.VMEM((nt, slots * rank, narrow + wide), BF16),
            pltpu.VMEM((stored, rows), BF16),
            dma((2,)),
            dma((2,)),
            dma((2,)),
            dma((n,)),
            dma((n, ng * nt)),
            dma(((n - 1) * max(mates - 1, 1),)),
            dma(((n - 1) * mates,)),
            dma((n,)),
            dma((n,)),
            dma((n,)),
            dma((n,)),
            dma((n,)),
            dma((n,)),
            dma((nt,)),
            dma((nt,)),
        ],
        compiler_params=pltpu.CompilerParams(
            collective_id=0, has_side_effects=True, vmem_limit_bytes=60 * 1024 * 1024
        ),
    )(tokens, w_flat, g_flat, a_all, b_all, want_rows)
    return (
        kv.reshape(rows, 2, part_cols),
        inp,
        ag.reshape(slots, rank, narrow),
        bg.reshape(slots, rank, 2, part_cols),
    )


def solution(mesh):
    in_specs = (
        P(("groups", "tenant"), None),
        P(None, None, "tensor"),
        P(("groups", "tenant"), None, "tensor"),
        P("tenant", None, "tensor"),
        P("tenant", None, None, "tensor"),
        P(("groups", "tenant")),
        P(),
    )
    out_specs = (
        P(("groups", "tenant"), None, "tensor"),
        P(("groups", "tenant"), "tensor"),
        P(("groups", "tenant"), None, "tensor"),
        P(("groups", "tenant"), None, None, "tensor"),
    )
    return jax.shard_map(local, mesh=mesh, in_specs=in_specs, out_specs=out_specs, check_vma=False)
```

```python
import functools
import jax
import jax.numpy as jnp
from jax import lax
from jax.experimental import pallas as pl
from jax.experimental.pallas import tpu as pltpu
from jax.sharding import PartitionSpec as P

F32 = jnp.float32
BF16 = jnp.bfloat16
MESH = pl.DeviceIdType.MESH


def mm(a, b, ca, cb):
    return lax.dot_general(a, b, (((ca,), (cb,)), ((), ())), preferred_element_type=F32)


def kernel(
    sizes, tokens, weight, g_ref, a_own, b_own, want_ref,
    kv_ref, in_ref, ag_ref, bg_ref,
    x_buf, wk_buf, acc, x_cols, w_buf, g_buf, total, rank_out, rank_in, grad_out, grad_in, back_ref, a_ref, b_ref,
    x_sem, wk_sem, own_sem, w_send, w_recv, plane_send, sib_send,
    up_send, up_recv, down_send, down_recv, rank_send, rank_recv, grad_send, grad_recv,
    a_send, a_recv, b_send, b_recv,
):
    n, ng, nt, piece, rank, step, parts = sizes
    rows, width = tokens.shape
    wide = weight.shape[1]
    narrow = x_cols.shape[1]
    stored = a_ref.shape[0]
    owned = stored // nt
    part_rows = rows // parts
    me = lax.axis_index("tensor")
    grp = lax.axis_index("groups")
    ten = lax.axis_index("tenant")
    plane = grp * nt + ten
    side = ten + 1 - 2 * lax.rem(ten, 2)

    def at_tensor(z):
        return (grp, ten, z)

    def line(k):
        return lax.rem(me + k, n)

    def mate(dg, dt):
        return lax.rem(grp + dg, ng), lax.rem(ten + dt, nt)

    barrier = pltpu.get_barrier_semaphore()
    for k in range(1, n):
        pl.semaphore_signal(barrier, inc=1, device_id=at_tensor(line(k)), device_id_type=MESH)
    for dg in range(ng):
        for dt in range(nt):
            if dg or dt:
                g2, t2 = mate(dg, dt)
                pl.semaphore_signal(barrier, inc=1, device_id=(g2, t2, me), device_id_type=MESH)

    def load(c, slot):
        return (
            pltpu.make_async_copy(
                tokens.at[:, pl.ds(pl.multiple_of(c * step, step), step)], x_buf.at[slot], x_sem.at[slot]
            ),
            pltpu.make_async_copy(
                weight.at[pl.ds(pl.multiple_of(c * step, step), step), :], wk_buf.at[slot], wk_sem.at[slot]
            ),
        )

    base = pl.multiple_of(me * narrow, narrow)
    own_x = pltpu.make_async_copy(tokens.at[:, pl.ds(base, narrow)], x_cols, own_sem.at[0])
    own_w = pltpu.make_async_copy(weight.at[pl.ds(base, narrow), :], w_buf.at[me], own_sem.at[1])
    own_x.start()
    for copy in load(0, 0):
        copy.start()
    own_w.start()

    def held(ref, t):
        return ref.at[pl.ds(pl.multiple_of(t * owned, owned), owned), :]

    held(a_ref, ten)[...] = a_own[...]
    held(b_ref, ten)[...] = b_own[...]
    pl.semaphore_wait(barrier, n - 1 + ng * nt - 1)

    def spot(z, p):
        return w_buf.at[z, pl.ds(pl.multiple_of(p * piece, piece), piece), :]

    def remote(src, dst, send, recv, device):
        return pltpu.make_async_remote_copy(
            src_ref=src, dst_ref=dst, send_sem=send, recv_sem=recv, device_id=device, device_id_type=MESH
        )

    adapter_sends = []

    def send_adapters(t, to, i):
        for ref, send, recv in ((a_ref, a_send, a_recv), (b_ref, b_send, b_recv)):
            copy = remote(held(ref, t), held(ref, t), send.at[i], recv.at[t], (grp, to, me))
            copy.start()
            adapter_sends.append(copy)

    def wait_adapters(t):
        for ref, send, recv in ((a_ref, a_send, a_recv), (b_ref, b_send, b_recv)):
            remote(held(ref, t), held(ref, t), send.at[0], recv.at[t], (grp, side, me)).wait_recv()

    send_adapters(ten, side, 0)
    for dt in range(2, nt, 2):
        send_adapters(ten, lax.rem(ten + dt, nt), dt)

    w_sends = []
    for k in range(1, n):
        z = line(k)
        start = pl.multiple_of(z * narrow + plane * piece, piece)
        copy = remote(
            weight.at[pl.ds(start, piece), :], spot(me, plane), w_send.at[k], w_recv.at[me, plane], at_tensor(z)
        )
        copy.start()
        w_sends.append(copy)

    def cut(ref, c):
        return ref.at[pl.ds(c * part_rows, part_rows), :]

    def hop(s, c, origin, to, send, recv):
        src = cut(g_ref, c) if s == 0 else cut(g_buf.at[origin], c)
        i = s * parts + c
        return remote(src, cut(g_buf.at[origin], c), send.at[i], recv.at[i], at_tensor(to))

    def up(s, c):
        copy = hop(s, c, jnp.maximum(me - s, 0), jnp.minimum(me + 1, n - 1), up_send, up_recv)
        return jnp.logical_and(me >= s, me < n - 1), copy

    def down(s, c):
        copy = hop(s, c, jnp.minimum(me + s, n - 1), jnp.maximum(me - 1, 0), down_send, down_recv)
        return jnp.logical_and(me + s < n, me > 0), copy

    def push(s, c):
        for ok, copy in (up(s, c), down(s, c)):
            pl.when(ok)(copy.start)

    def arrived(s, c):
        low, high = me - 1 - s, me + 1 + s
        pl.when(low >= 0)(
            hop(s, c, jnp.maximum(low, 0), jnp.maximum(me - 1, 0), up_send, up_recv).wait_recv
        )
        pl.when(high < n)(
            hop(s, c, jnp.minimum(high, n - 1), jnp.minimum(me + 1, n - 1), down_send, down_recv).wait_recv
        )

    def relay(s):
        for c in range(parts):
            arrived(s, c)
            push(s + 1, c)

    for c in range(parts):
        push(0, c)

    chunks = width // step
    acc[...] = jnp.zeros_like(acc)

    def chunk(c, carry):
        slot = lax.rem(c, 2)

        @pl.when(c + 1 < chunks)
        def _():
            for copy in load(c + 1, 1 - slot):
                copy.start()

        for copy in load(c, slot):
            copy.wait()
        acc[...] += mm(x_buf[slot], wk_buf[slot], 1, 0)
        return carry

    half = chunks // 2
    lax.fori_loop(0, half, chunk, 0)
    for dt in range(2, nt, 2):
        t2 = lax.rem(ten + dt, nt)
        wait_adapters(t2)
        send_adapters(t2, side, dt + 1)
    lax.fori_loop(half, chunks, chunk, 0)
    for dt in range(0, nt, 2):
        wait_adapters(lax.rem(side + dt, nt))

    ids = lax.broadcasted_iota(jnp.int32, (stored, 1), 0) // rank
    mask = ids == want_ref[...]
    fold = (
        lax.rem(lax.broadcasted_iota(jnp.int32, (stored, rank), 0), rank)
        == lax.broadcasted_iota(jnp.int32, (stored, rank), 1)
    ).astype(BF16)
    own_x.wait()
    part = jnp.where(mask, mm(a_ref[...], x_cols[...], 1, 1), 0.0).astype(BF16)
    rank_out[:rank, :] = mm(fold, part, 0, 0).astype(BF16)
    part = jnp.where(mask, mm(b_ref[...], g_ref[...], 1, 1), 0.0).astype(BF16)
    rank_out[rank:, :] = mm(fold, part, 0, 0).astype(BF16)
    rank_sends = []
    for k in range(1, n):
        copy = remote(rank_out, rank_in.at[me], rank_send.at[k], rank_recv.at[me], at_tensor(line(k)))
        copy.start()
        rank_sends.append(copy)

    tile = min(narrow, 512)

    def add_block(o, g_block, first):
        def body(c, carry):
            cols = pl.ds(pl.multiple_of(c * tile, tile), tile)
            term = mm(g_block[...], w_buf[o, cols, :], 1, 1)
            if first:
                total[:, cols] = term
            else:
                total[:, cols] += term
            return carry

        lax.fori_loop(0, narrow // tile, body, 0)

    own_w.wait()
    add_block(me, g_ref, True)

    plane_sends, sib_sends = [], []

    def to_side(z, p, i):
        copy = remote(spot(z, p), spot(z, p), sib_send.at[i], w_recv.at[z, p], (grp, side, me))
        copy.start()
        sib_sends.append(copy)

    def wait_piece(z, p):
        remote(spot(z, p), spot(z, p), sib_send.at[0], w_recv.at[z, p], (grp, side, me)).wait_recv()

    others = [(dg, dt) for dg in range(ng) for dt in range(0, nt, 2) if dg or dt]
    near = sorted(range(1, n), key=lambda k: (min(k, n - k), k))
    for k in near:
        z = line(k)
        wait_piece(z, plane)
        for dg, dt in others:
            g2, t2 = mate(dg, dt)
            copy = remote(
                spot(z, plane), spot(z, plane), plane_send.at[len(plane_sends)], w_recv.at[z, plane], (g2, t2, me)
            )
            copy.start()
            plane_sends.append(copy)
        to_side(z, plane, len(sib_sends))

    rank_in[me] = rank_out[...]
    for k in range(1, n):
        z = line(k)
        remote(rank_out, rank_in.at[z], rank_send.at[k], rank_recv.at[z], at_tensor(z)).wait_recv()
    whole = rank_in[0].astype(F32)
    for z in range(1, n):
        whole = whole + rank_in[z].astype(F32)
    twice = (whole.astype(BF16).astype(F32) * 2.0).astype(BF16)
    shrink = jnp.where(mask, mm(fold, twice[:rank, :], 1, 0), 0.0).astype(BF16)
    back_ref[...] = jnp.where(mask, mm(fold, twice[rank:, :], 1, 0), 0.0).astype(BF16)

    if n > 2:
        relay(0)
    for p in range(nt):
        grad_out[p, :, :narrow] = mm(back_ref[pl.ds(p * owned, owned), :], x_cols[...], 1, 0).astype(BF16)
    spread = mm(shrink, g_ref[...], 1, 0).astype(BF16)
    for p in range(nt):
        grad_out[p, :, narrow:] = spread[p * owned : (p + 1) * owned, :]
    grad_sends = []
    for dt in range(1, nt):
        t2 = lax.rem(ten + dt, nt)
        copy = remote(grad_out.at[t2], grad_in.at[ten], grad_send.at[dt], grad_recv.at[ten], (grp, t2, me))
        copy.start()
        grad_sends.append(copy)
    kv_ref[...] = (acc[...] + mm(shrink, b_ref[...], 0, 0)).astype(BF16)

    def add_adapter(c, carry):
        cols = pl.ds(pl.multiple_of(c * tile, tile), tile)
        total[:, cols] += mm(back_ref[...], a_ref[:, cols], 0, 0)
        return carry

    lax.fori_loop(0, narrow // tile, add_adapter, 0)
    for k in near:
        z = line(k)
        for dg, dt in others:
            g2, t2 = mate(dg, dt)
            p = g2 * nt + t2
            wait_piece(z, p)
            to_side(z, p, len(sib_sends))
    for s in range(1, n - 2):
        relay(s)
    for k in range(1, n):
        z = line(k)
        for dg in range(ng):
            for dt in range(0, nt, 2):
                g2 = lax.rem(grp + dg, ng)
                t2 = lax.rem(side + dt, nt)
                wait_piece(z, g2 * nt + t2)

    def use(s):
        low, high = me - 1 - s, me + 1 + s

        @pl.when(low >= 0)
        def _():
            o = jnp.maximum(low, 0)
            add_block(o, g_buf.at[o], False)

        @pl.when(high < n)
        def _():
            o = jnp.minimum(high, n - 1)
            add_block(o, g_buf.at[o], False)

    for s in range(n - 2):
        use(s)

    grad_in[ten] = grad_out[ten]
    for dt in range(1, nt):
        t2 = lax.rem(ten + dt, nt)
        remote(grad_out.at[t2], grad_in.at[t2], grad_send.at[dt], grad_recv.at[t2], (grp, t2, me)).wait_recv()
    ag = grad_in[0, :, :narrow].astype(F32)
    bg = grad_in[0, :, narrow:].astype(F32)
    for p in range(1, nt):
        ag = ag + grad_in[p, :, :narrow].astype(F32)
        bg = bg + grad_in[p, :, narrow:].astype(F32)
    ag_ref[...] = ag
    bg_ref[...] = bg

    def finish(o):
        for c in range(parts):
            arrived(n - 2, c)
            span = pl.ds(c * part_rows, part_rows)

            def body(i, carry):
                cols = pl.ds(pl.multiple_of(i * tile, tile), tile)
                term = mm(g_buf[o, span, :], w_buf[o, cols, :], 1, 1)
                in_ref[span, cols] = (total[span, cols] + term).astype(BF16)
                return carry

            lax.fori_loop(0, narrow // tile, body, 0)

    pl.when(me == n - 1)(lambda: finish(0))
    pl.when(me == 0)(lambda: finish(n - 1))

    @pl.when(jnp.logical_and(me > 0, me < n - 1))
    def _():
        in_ref[...] = total[...].astype(BF16)

    for copy in w_sends + plane_sends + sib_sends + rank_sends + grad_sends + adapter_sends:
        copy.wait_send()
    for s in range(n - 1):
        for c in range(parts):
            for ok, copy in (up(s, c), down(s, c)):
                pl.when(ok)(copy.wait_send)


def local(tokens, kv_weight, cotangent, a_store, b_store, tile_tenant, tenant_place):
    rows, model_width = tokens.shape
    tiles = tile_tenant.shape[0]
    tile_len = rows // tiles
    slots, rank, narrow = a_store.shape
    part_cols = kv_weight.shape[2]
    wide = 2 * part_cols
    tenants = tenant_place.shape[0]
    n = lax.axis_size("tensor")
    nt = lax.axis_size("tenant")
    ng = lax.axis_size("groups")
    piece = narrow // (ng * nt)

    stored = nt * slots * rank
    w_flat = kv_weight.reshape(model_width, wide)
    g_flat = cotangent.reshape(rows, wide)
    lookup = tile_tenant[:, None] == jnp.arange(tenants, dtype=jnp.int32)[None, :]
    wanted = jnp.sum(jnp.where(lookup, tenant_place[None, :], 0), axis=1)
    want_rows = jnp.repeat(wanted, tile_len)[None, :]

    step = 1024 if model_width % 1024 == 0 else model_width // 2
    vmem = pl.BlockSpec(memory_space=pltpu.VMEM)
    hbm = pl.BlockSpec(memory_space=pl.ANY)
    dma = pltpu.SemaphoreType.DMA
    mates = ng * nt // 2
    parts = 2
    kv, inp, ag, bg = pl.pallas_call(
        functools.partial(kernel, (n, ng, nt, piece, rank, step, parts)),
        out_shape=(
            jax.ShapeDtypeStruct((rows, wide), BF16),
            jax.ShapeDtypeStruct((rows, narrow), BF16),
            jax.ShapeDtypeStruct((slots * rank, narrow), F32),
            jax.ShapeDtypeStruct((slots * rank, wide), F32),
        ),
        in_specs=[hbm, hbm, vmem, vmem, vmem, vmem],
        out_specs=(vmem, vmem, vmem, vmem),
        scratch_shapes=[
            pltpu.VMEM((2, rows, step), BF16),
            pltpu.VMEM((2, step, wide), BF16),
            pltpu.VMEM((rows, wide), F32),
            pltpu.VMEM((rows, narrow), BF16),
            pltpu.VMEM((n, narrow, wide), BF16),
            pltpu.VMEM((n, rows, wide), BF16),
            pltpu.VMEM((rows, narrow), F32),
            pltpu.VMEM((2 * rank, rows), BF16),
            pltpu.VMEM((n, 2 * rank, rows), BF16),
            pltpu.VMEM((nt, slots * rank, narrow + wide), BF16),
            pltpu.VMEM((nt, slots * rank, narrow + wide), BF16),
            pltpu.VMEM((stored, rows), BF16),
            pltpu.VMEM((stored, narrow), BF16),
            pltpu.VMEM((stored, wide), BF16),
            dma((2,)),
            dma((2,)),
            dma((2,)),
            dma((n,)),
            dma((n, ng * nt)),
            dma(((n - 1) * max(mates - 1, 1),)),
            dma(((n - 1) * mates,)),
            dma((n * parts,)),
            dma((n * parts,)),
            dma((n * parts,)),
            dma((n * parts,)),
            dma((n,)),
            dma((n,)),
            dma((nt,)),
            dma((nt,)),
            dma((nt,)),
            dma((nt,)),
            dma((nt,)),
            dma((nt,)),
        ],
        compiler_params=pltpu.CompilerParams(
            collective_id=0, has_side_effects=True, vmem_limit_bytes=60 * 1024 * 1024
        ),
    )(
        tokens,
        w_flat,
        g_flat,
        a_store.reshape(slots * rank, narrow),
        b_store.reshape(slots * rank, wide),
        want_rows,
    )
    return (
        kv.reshape(rows, 2, part_cols),
        inp,
        ag.reshape(slots, rank, narrow),
        bg.reshape(slots, rank, 2, part_cols),
    )


def solution(mesh):
    in_specs = (
        P(("groups", "tenant"), None),
        P(None, None, "tensor"),
        P(("groups", "tenant"), None, "tensor"),
        P("tenant", None, "tensor"),
        P("tenant", None, None, "tensor"),
        P(("groups", "tenant")),
        P(),
    )
    out_specs = (
        P(("groups", "tenant"), None, "tensor"),
        P(("groups", "tenant"), "tensor"),
        P(("groups", "tenant"), None, "tensor"),
        P(("groups", "tenant"), None, None, "tensor"),
    )
    return jax.shard_map(local, mesh=mesh, in_specs=in_specs, out_specs=out_specs, check_vma=False)
```

```python
import functools
import jax
import jax.numpy as jnp
from jax import lax
from jax.experimental import pallas as pl
from jax.experimental.pallas import tpu as pltpu
from jax.sharding import PartitionSpec as P

F32 = jnp.float32
BF16 = jnp.bfloat16
MESH = pl.DeviceIdType.MESH


def mm(a, b, ca, cb):
    return lax.dot_general(a, b, (((ca,), (cb,)), ((), ())), preferred_element_type=F32)


def kernel(
    sizes, tokens, weight, g_ref, a_own, b_own, want_ref,
    kv_ref, in_ref, ag_ref, bg_ref,
    x_buf, wk_buf, acc, x_cols, w_buf, g_buf, total, rank_out, rank_in, grad_out, grad_side, grad_in, back_ref, a_ref, b_ref,
    x_sem, wk_sem, own_sem, w_send, w_recv, plane_send, sib_send,
    up_send, up_recv, down_send, down_recv, rank_send, rank_recv, grad_send, grad_recv,
    a_send, a_recv, b_send, b_recv, side_recv,
):
    n, ng, nt, piece, rank, step, parts = sizes
    rows, width = tokens.shape
    wide = weight.shape[1]
    narrow = x_cols.shape[1]
    stored = a_ref.shape[0]
    owned = stored // nt
    part_rows = rows // parts
    me = lax.axis_index("tensor")
    grp = lax.axis_index("groups")
    ten = lax.axis_index("tenant")
    plane = grp * nt + ten
    side = ten + 1 - 2 * lax.rem(ten, 2)

    def at_tensor(z):
        return (grp, ten, z)

    def line(k):
        return lax.rem(me + k, n)

    def mate(dg, dt):
        return lax.rem(grp + dg, ng), lax.rem(ten + dt, nt)

    barrier = pltpu.get_barrier_semaphore()
    for k in range(1, n):
        pl.semaphore_signal(barrier, inc=1, device_id=at_tensor(line(k)), device_id_type=MESH)
    for dg in range(ng):
        for dt in range(nt):
            if dg or dt:
                g2, t2 = mate(dg, dt)
                pl.semaphore_signal(barrier, inc=1, device_id=(g2, t2, me), device_id_type=MESH)

    def load(c, slot):
        return (
            pltpu.make_async_copy(
                tokens.at[:, pl.ds(pl.multiple_of(c * step, step), step)], x_buf.at[slot], x_sem.at[slot]
            ),
            pltpu.make_async_copy(
                weight.at[pl.ds(pl.multiple_of(c * step, step), step), :], wk_buf.at[slot], wk_sem.at[slot]
            ),
        )

    base = pl.multiple_of(me * narrow, narrow)
    own_x = pltpu.make_async_copy(tokens.at[:, pl.ds(base, narrow)], x_cols, own_sem.at[0])
    own_w = pltpu.make_async_copy(weight.at[pl.ds(base, narrow), :], w_buf.at[me], own_sem.at[1])
    own_x.start()
    for copy in load(0, 0):
        copy.start()
    own_w.start()

    def held(ref, t):
        return ref.at[pl.ds(pl.multiple_of(t * owned, owned), owned), :]

    held(a_ref, ten)[...] = a_own[...]
    held(b_ref, ten)[...] = b_own[...]
    pl.semaphore_wait(barrier, n - 1 + ng * nt - 1)

    def spot(z, p):
        return w_buf.at[z, pl.ds(pl.multiple_of(p * piece, piece), piece), :]

    def remote(src, dst, send, recv, device):
        return pltpu.make_async_remote_copy(
            src_ref=src, dst_ref=dst, send_sem=send, recv_sem=recv, device_id=device, device_id_type=MESH
        )

    adapter_sends = []

    def send_adapters(t, to, i):
        for ref, send, recv in ((a_ref, a_send, a_recv), (b_ref, b_send, b_recv)):
            copy = remote(held(ref, t), held(ref, t), send.at[i], recv.at[t], (grp, to, me))
            copy.start()
            adapter_sends.append(copy)

    def wait_adapters(t):
        for ref, send, recv in ((a_ref, a_send, a_recv), (b_ref, b_send, b_recv)):
            remote(held(ref, t), held(ref, t), send.at[0], recv.at[t], (grp, side, me)).wait_recv()

    send_adapters(ten, side, 0)
    for dt in range(2, nt, 2):
        send_adapters(ten, lax.rem(ten + dt, nt), dt)

    w_sends = []
    for k in range(1, n):
        z = line(k)
        start = pl.multiple_of(z * narrow + plane * piece, piece)
        copy = remote(
            weight.at[pl.ds(start, piece), :], spot(me, plane), w_send.at[k], w_recv.at[me, plane], at_tensor(z)
        )
        copy.start()
        w_sends.append(copy)

    def cut(ref, c):
        return ref.at[pl.ds(c * part_rows, part_rows), :]

    def hop(s, c, origin, to, send, recv):
        src = cut(g_ref, c) if s == 0 else cut(g_buf.at[origin], c)
        i = s * parts + c
        return remote(src, cut(g_buf.at[origin], c), send.at[i], recv.at[i], at_tensor(to))

    def up(s, c):
        copy = hop(s, c, jnp.maximum(me - s, 0), jnp.minimum(me + 1, n - 1), up_send, up_recv)
        return jnp.logical_and(me >= s, me < n - 1), copy

    def down(s, c):
        copy = hop(s, c, jnp.minimum(me + s, n - 1), jnp.maximum(me - 1, 0), down_send, down_recv)
        return jnp.logical_and(me + s < n, me > 0), copy

    def push(s, c):
        for ok, copy in (up(s, c), down(s, c)):
            pl.when(ok)(copy.start)

    def arrived(s, c):
        low, high = me - 1 - s, me + 1 + s
        pl.when(low >= 0)(
            hop(s, c, jnp.maximum(low, 0), jnp.maximum(me - 1, 0), up_send, up_recv).wait_recv
        )
        pl.when(high < n)(
            hop(s, c, jnp.minimum(high, n - 1), jnp.minimum(me + 1, n - 1), down_send, down_recv).wait_recv
        )

    def relay(s):
        for c in range(parts):
            arrived(s, c)
            push(s + 1, c)

    others = [(dg, dt) for dg in range(ng) for dt in range(0, nt, 2) if dg or dt]

    def to_side(z, p, i):
        return remote(spot(z, p), spot(z, p), sib_send.at[i], w_recv.at[z, p], (grp, side, me))

    def wait_piece(z, p):
        to_side(z, p, 0).wait_recv()

    def fan_out(z):
        turn = lax.rem(z - me + n, n) - 1
        copies = [to_side(z, plane, turn * (len(others) + 1))]
        for i, (dg, dt) in enumerate(others):
            g2, t2 = mate(dg, dt)
            copies.append(
                remote(
                    spot(z, plane), spot(z, plane), plane_send.at[turn * len(others) + i], w_recv.at[z, plane], (g2, t2, me)
                )
            )
        return copies

    def pass_on(z):
        turn = lax.rem(z - me + n, n) - 1
        found = []
        for i, (dg, dt) in enumerate(others):
            g2, t2 = mate(dg, dt)
            p = g2 * nt + t2
            found.append((p, to_side(z, p, turn * (len(others) + 1) + 1 + i)))
        return found

    def both(distance, act):
        low, high = me - distance, me + distance
        pl.when(low >= 0)(lambda: act(jnp.maximum(low, 0)))
        pl.when(high < n)(lambda: act(jnp.minimum(high, n - 1)))

    def fan(z):
        wait_piece(z, plane)
        for copy in fan_out(z)[::-1]:
            copy.start()

    def hand(z):
        for p, copy in pass_on(z):
            wait_piece(z, p)
            copy.start()

    def settle(z):
        for dg in range(ng):
            for dt in range(0, nt, 2):
                wait_piece(z, lax.rem(grp + dg, ng) * nt + lax.rem(side + dt, nt))

    chunks = width // step
    acc[...] = jnp.zeros_like(acc)

    def chunk(c, carry):
        slot = lax.rem(c, 2)

        @pl.when(c + 1 < chunks)
        def _():
            for copy in load(c + 1, 1 - slot):
                copy.start()

        for copy in load(c, slot):
            copy.wait()
        acc[...] += mm(x_buf[slot], wk_buf[slot], 1, 0)
        return carry

    half = chunks // 2
    lax.fori_loop(0, half, chunk, 0)
    for dt in range(2, nt, 2):
        t2 = lax.rem(ten + dt, nt)
        wait_adapters(t2)
        send_adapters(t2, side, dt + 1)
    for c in range(parts):
        push(0, c)
    both(1, fan)
    lax.fori_loop(half, chunks, chunk, 0)
    if n > 2:
        both(2, fan)
    for dt in range(0, nt, 2):
        wait_adapters(lax.rem(side + dt, nt))

    ids = lax.broadcasted_iota(jnp.int32, (stored, 1), 0) // rank
    mask = ids == want_ref[...]
    fold = (
        lax.rem(lax.broadcasted_iota(jnp.int32, (stored, rank), 0), rank)
        == lax.broadcasted_iota(jnp.int32, (stored, rank), 1)
    ).astype(BF16)
    own_x.wait()
    part = jnp.where(mask, mm(a_ref[...], x_cols[...], 1, 1), 0.0).astype(BF16)
    rank_out[:rank, :] = mm(fold, part, 0, 0).astype(BF16)
    part = jnp.where(mask, mm(b_ref[...], g_ref[...], 1, 1), 0.0).astype(BF16)
    rank_out[rank:, :] = mm(fold, part, 0, 0).astype(BF16)
    rank_sends = []
    for k in range(1, n):
        copy = remote(rank_out, rank_in.at[me], rank_send.at[k], rank_recv.at[me], at_tensor(line(k)))
        copy.start()
        rank_sends.append(copy)

    tile = min(narrow, 512)

    def add_block(o, g_block, first):
        def body(c, carry):
            cols = pl.ds(pl.multiple_of(c * tile, tile), tile)
            term = mm(g_block[...], w_buf[o, cols, :], 1, 1)
            if first:
                total[:, cols] = term
            else:
                total[:, cols] += term
            return carry

        lax.fori_loop(0, narrow // tile, body, 0)

    for d in range(3, n):
        both(d, fan)
    own_w.wait()
    add_block(me, g_ref, True)
    both(1, hand)

    rank_in[me] = rank_out[...]
    for k in range(1, n):
        z = line(k)
        remote(rank_out, rank_in.at[z], rank_send.at[k], rank_recv.at[z], at_tensor(z)).wait_recv()
    whole = rank_in[0].astype(F32)
    for z in range(1, n):
        whole = whole + rank_in[z].astype(F32)
    twice = (whole.astype(BF16).astype(F32) * 2.0).astype(BF16)
    shrink = jnp.where(mask, mm(fold, twice[:rank, :], 1, 0), 0.0).astype(BF16)
    back_ref[...] = jnp.where(mask, mm(fold, twice[rank:, :], 1, 0), 0.0).astype(BF16)

    for p in range(nt):
        grad_out[p, :, :narrow] = mm(back_ref[pl.ds(p * owned, owned), :], x_cols[...], 1, 0).astype(BF16)
    spread = mm(shrink, g_ref[...], 1, 0).astype(BF16)
    for p in range(nt):
        grad_out[p, :, narrow:] = spread[p * owned : (p + 1) * owned, :]
    grad_sends = []
    for dt in range(0, nt, 2):
        t2 = lax.rem(side + dt, nt)
        copy = remote(grad_out.at[t2], grad_side.at[t2], grad_send.at[dt], side_recv.at[t2], (grp, side, me))
        copy.start()
        grad_sends.append(copy)
    kv_ref[...] = (acc[...] + mm(shrink, b_ref[...], 0, 0)).astype(BF16)

    if n > 2:
        relay(0)
    for dt in range(0, nt, 2):
        t2 = lax.rem(ten + dt, nt)
        remote(grad_out.at[t2], grad_side.at[t2], grad_send.at[0], side_recv.at[t2], (grp, side, me)).wait_recv()
        if dt:
            grad_out[t2] = (grad_out[t2].astype(F32) + grad_side[t2].astype(F32)).astype(BF16)
            copy = remote(grad_out.at[t2], grad_in.at[ten], grad_send.at[dt + 1], grad_recv.at[ten], (grp, t2, me))
            copy.start()
            grad_sends.append(copy)

    def add_adapter(c, carry):
        cols = pl.ds(pl.multiple_of(c * tile, tile), tile)
        total[:, cols] += mm(back_ref[...], a_ref[:, cols], 0, 0)
        return carry

    lax.fori_loop(0, narrow // tile, add_adapter, 0)
    def use(s):
        low, high = me - 1 - s, me + 1 + s

        @pl.when(low >= 0)
        def _():
            o = jnp.maximum(low, 0)
            add_block(o, g_buf.at[o], False)

        @pl.when(high < n)
        def _():
            o = jnp.minimum(high, n - 1)
            add_block(o, g_buf.at[o], False)

    for d in range(2, n):
        both(d, hand)
    for s in range(n - 2):
        if s:
            relay(s)
        both(s + 1, settle)
        use(s)

    ag = grad_out[ten, :, :narrow].astype(F32) + grad_side[ten, :, :narrow].astype(F32)
    bg = grad_out[ten, :, narrow:].astype(F32) + grad_side[ten, :, narrow:].astype(F32)
    for dt in range(2, nt, 2):
        t2 = lax.rem(ten + dt, nt)
        remote(grad_out.at[t2], grad_in.at[t2], grad_send.at[0], grad_recv.at[t2], (grp, t2, me)).wait_recv()
        ag = ag + grad_in[t2, :, :narrow].astype(F32)
        bg = bg + grad_in[t2, :, narrow:].astype(F32)
    ag_ref[...] = ag
    bg_ref[...] = bg

    both(n - 1, settle)

    def finish(o):
        for c in range(parts):
            arrived(n - 2, c)
            span = pl.ds(c * part_rows, part_rows)

            def body(i, carry):
                cols = pl.ds(pl.multiple_of(i * tile, tile), tile)
                term = mm(g_buf[o, span, :], w_buf[o, cols, :], 1, 1)
                in_ref[span, cols] = (total[span, cols] + term).astype(BF16)
                return carry

            lax.fori_loop(0, narrow // tile, body, 0)

    pl.when(me == n - 1)(lambda: finish(0))
    pl.when(me == 0)(lambda: finish(n - 1))

    @pl.when(jnp.logical_and(me > 0, me < n - 1))
    def _():
        in_ref[...] = total[...].astype(BF16)

    for k in range(1, n):
        z = line(k)
        for copy in fan_out(z) + [copy for _, copy in pass_on(z)]:
            copy.wait_send()
    for copy in w_sends + rank_sends + grad_sends + adapter_sends:
        copy.wait_send()
    for s in range(n - 1):
        for c in range(parts):
            for ok, copy in (up(s, c), down(s, c)):
                pl.when(ok)(copy.wait_send)


def local(tokens, kv_weight, cotangent, a_store, b_store, tile_tenant, tenant_place):
    rows, model_width = tokens.shape
    tiles = tile_tenant.shape[0]
    tile_len = rows // tiles
    slots, rank, narrow = a_store.shape
    part_cols = kv_weight.shape[2]
    wide = 2 * part_cols
    tenants = tenant_place.shape[0]
    n = lax.axis_size("tensor")
    nt = lax.axis_size("tenant")
    ng = lax.axis_size("groups")
    piece = narrow // (ng * nt)

    stored = nt * slots * rank
    w_flat = kv_weight.reshape(model_width, wide)
    g_flat = cotangent.reshape(rows, wide)
    lookup = tile_tenant[:, None] == jnp.arange(tenants, dtype=jnp.int32)[None, :]
    wanted = jnp.sum(jnp.where(lookup, tenant_place[None, :], 0), axis=1)
    want_rows = jnp.repeat(wanted, tile_len)[None, :]

    step = 1024 if model_width % 1024 == 0 else model_width // 2
    vmem = pl.BlockSpec(memory_space=pltpu.VMEM)
    hbm = pl.BlockSpec(memory_space=pl.ANY)
    dma = pltpu.SemaphoreType.DMA
    mates = ng * nt // 2
    parts = 2
    kv, inp, ag, bg = pl.pallas_call(
        functools.partial(kernel, (n, ng, nt, piece, rank, step, parts)),
        out_shape=(
            jax.ShapeDtypeStruct((rows, wide), BF16),
            jax.ShapeDtypeStruct((rows, narrow), BF16),
            jax.ShapeDtypeStruct((slots * rank, narrow), F32),
            jax.ShapeDtypeStruct((slots * rank, wide), F32),
        ),
        in_specs=[hbm, hbm, vmem, vmem, vmem, vmem],
        out_specs=(vmem, vmem, vmem, vmem),
        scratch_shapes=[
            pltpu.VMEM((2, rows, step), BF16),
            pltpu.VMEM((2, step, wide), BF16),
            pltpu.VMEM((rows, wide), F32),
            pltpu.VMEM((rows, narrow), BF16),
            pltpu.VMEM((n, narrow, wide), BF16),
            pltpu.VMEM((n, rows, wide), BF16),
            pltpu.VMEM((rows, narrow), F32),
            pltpu.VMEM((2 * rank, rows), BF16),
            pltpu.VMEM((n, 2 * rank, rows), BF16),
            pltpu.VMEM((nt, slots * rank, narrow + wide), BF16),
            pltpu.VMEM((nt, slots * rank, narrow + wide), BF16),
            pltpu.VMEM((nt, slots * rank, narrow + wide), BF16),
            pltpu.VMEM((stored, rows), BF16),
            pltpu.VMEM((stored, narrow), BF16),
            pltpu.VMEM((stored, wide), BF16),
            dma((2,)),
            dma((2,)),
            dma((2,)),
            dma((n,)),
            dma((n, ng * nt)),
            dma(((n - 1) * max(mates - 1, 1),)),
            dma(((n - 1) * mates,)),
            dma((n * parts,)),
            dma((n * parts,)),
            dma((n * parts,)),
            dma((n * parts,)),
            dma((n,)),
            dma((n,)),
            dma((nt,)),
            dma((nt,)),
            dma((nt,)),
            dma((nt,)),
            dma((nt,)),
            dma((nt,)),
            dma((nt,)),
        ],
        compiler_params=pltpu.CompilerParams(
            collective_id=0, has_side_effects=True, vmem_limit_bytes=60 * 1024 * 1024
        ),
    )(
        tokens,
        w_flat,
        g_flat,
        a_store.reshape(slots * rank, narrow),
        b_store.reshape(slots * rank, wide),
        want_rows,
    )
    return (
        kv.reshape(rows, 2, part_cols),
        inp,
        ag.reshape(slots, rank, narrow),
        bg.reshape(slots, rank, 2, part_cols),
    )


def solution(mesh):
    in_specs = (
        P(("groups", "tenant"), None),
        P(None, None, "tensor"),
        P(("groups", "tenant"), None, "tensor"),
        P("tenant", None, "tensor"),
        P("tenant", None, None, "tensor"),
        P(("groups", "tenant")),
        P(),
    )
    out_specs = (
        P(("groups", "tenant"), None, "tensor"),
        P(("groups", "tenant"), "tensor"),
        P(("groups", "tenant"), None, "tensor"),
        P(("groups", "tenant"), None, None, "tensor"),
    )
    return jax.shard_map(local, mesh=mesh, in_specs=in_specs, out_specs=out_specs, check_vma=False)
```

```python
import functools
import jax
import jax.numpy as jnp
from jax import lax
from jax.experimental import pallas as pl
from jax.experimental.pallas import tpu as pltpu
from jax.sharding import PartitionSpec as P

F32 = jnp.float32
BF16 = jnp.bfloat16
MESH = pl.DeviceIdType.MESH


def mm(a, b, ca, cb):
    return lax.dot_general(a, b, (((ca,), (cb,)), ((), ())), preferred_element_type=F32)


def kernel(
    sizes, tokens, weight, g_ref, a_own, b_own, want_ref,
    kv_ref, in_ref, ag_ref, bg_ref,
    x_buf, wk_buf, acc, x_cols, w_buf, g_buf, total, rank_out, rank_in, grad_out, grad_side, grad_in, back_ref, a_ref, b_ref,
    x_sem, wk_sem, own_sem, w_send, w_recv, plane_send, sib_send,
    up_send, up_recv, down_send, down_recv, rank_send, rank_recv, grad_send, grad_recv,
    a_send, a_recv, b_send, b_recv, side_recv,
):
    n, ng, nt, piece, rank, step, parts = sizes
    rows, width = tokens.shape
    wide = weight.shape[1]
    narrow = x_cols.shape[1]
    stored = a_ref.shape[0]
    owned = stored // nt
    part_rows = rows // parts
    me = lax.axis_index("tensor")
    grp = lax.axis_index("groups")
    ten = lax.axis_index("tenant")
    plane = grp * nt + ten
    side = ten + 1 - 2 * lax.rem(ten, 2)

    def at_tensor(z):
        return (grp, ten, z)

    def line(k):
        return lax.rem(me + k, n)

    def mate(dg, dt):
        return lax.rem(grp + dg, ng), lax.rem(ten + dt, nt)

    barrier = pltpu.get_barrier_semaphore()
    for k in range(1, n):
        pl.semaphore_signal(barrier, inc=1, device_id=at_tensor(line(k)), device_id_type=MESH)
    for dg in range(ng):
        for dt in range(nt):
            if dg or dt:
                g2, t2 = mate(dg, dt)
                pl.semaphore_signal(barrier, inc=1, device_id=(g2, t2, me), device_id_type=MESH)

    def load(c, slot):
        return (
            pltpu.make_async_copy(
                tokens.at[:, pl.ds(pl.multiple_of(c * step, step), step)], x_buf.at[slot], x_sem.at[slot]
            ),
            pltpu.make_async_copy(
                weight.at[pl.ds(pl.multiple_of(c * step, step), step), :], wk_buf.at[slot], wk_sem.at[slot]
            ),
        )

    base = pl.multiple_of(me * narrow, narrow)
    own_x = pltpu.make_async_copy(tokens.at[:, pl.ds(base, narrow)], x_cols, own_sem.at[0])
    own_w = pltpu.make_async_copy(weight.at[pl.ds(base, narrow), :], w_buf.at[me], own_sem.at[1])
    own_x.start()
    for copy in load(0, 0):
        copy.start()
    own_w.start()

    def held(ref, t):
        return ref.at[pl.ds(pl.multiple_of(t * owned, owned), owned), :]

    held(a_ref, ten)[...] = a_own[...]
    held(b_ref, ten)[...] = b_own[...]
    pl.semaphore_wait(barrier, n - 1 + ng * nt - 1)

    def spot(z, p):
        return w_buf.at[z, pl.ds(pl.multiple_of(p * piece, piece), piece), :]

    def remote(src, dst, send, recv, device):
        return pltpu.make_async_remote_copy(
            src_ref=src, dst_ref=dst, send_sem=send, recv_sem=recv, device_id=device, device_id_type=MESH
        )

    adapter_sends = []

    def send_adapters(t, to, i):
        for ref, send, recv in ((a_ref, a_send, a_recv), (b_ref, b_send, b_recv)):
            copy = remote(held(ref, t), held(ref, t), send.at[i], recv.at[t], (grp, to, me))
            copy.start()
            adapter_sends.append(copy)

    def wait_adapters(t):
        for ref, send, recv in ((a_ref, a_send, a_recv), (b_ref, b_send, b_recv)):
            remote(held(ref, t), held(ref, t), send.at[0], recv.at[t], (grp, side, me)).wait_recv()

    send_adapters(ten, side, 0)
    for dt in range(2, nt, 2):
        send_adapters(ten, lax.rem(ten + dt, nt), dt)

    w_sends = []
    for k in range(1, n):
        z = line(k)
        start = pl.multiple_of(z * narrow + plane * piece, piece)
        copy = remote(
            weight.at[pl.ds(start, piece), :], spot(me, plane), w_send.at[k], w_recv.at[me, plane], at_tensor(z)
        )
        copy.start()
        w_sends.append(copy)

    def cut(ref, c):
        return ref.at[pl.ds(c * part_rows, part_rows), :]

    def hop(s, c, origin, to, send, recv):
        src = cut(g_ref, c) if s == 0 else cut(g_buf.at[origin], c)
        i = s * parts + c
        return remote(src, cut(g_buf.at[origin], c), send.at[i], recv.at[i], at_tensor(to))

    def up(s, c):
        copy = hop(s, c, jnp.maximum(me - s, 0), jnp.minimum(me + 1, n - 1), up_send, up_recv)
        return jnp.logical_and(me >= s, me < n - 1), copy

    def down(s, c):
        copy = hop(s, c, jnp.minimum(me + s, n - 1), jnp.maximum(me - 1, 0), down_send, down_recv)
        return jnp.logical_and(me + s < n, me > 0), copy

    def push(s, c):
        for ok, copy in (up(s, c), down(s, c)):
            pl.when(ok)(copy.start)

    def arrived(s, c):
        low, high = me - 1 - s, me + 1 + s
        pl.when(low >= 0)(
            hop(s, c, jnp.maximum(low, 0), jnp.maximum(me - 1, 0), up_send, up_recv).wait_recv
        )
        pl.when(high < n)(
            hop(s, c, jnp.minimum(high, n - 1), jnp.minimum(me + 1, n - 1), down_send, down_recv).wait_recv
        )

    def relay(s):
        for c in range(parts):
            arrived(s, c)
            push(s + 1, c)

    for c in range(parts):
        push(0, c)

    others = [(dg, dt) for dg in range(ng) for dt in range(0, nt, 2) if dg or dt]

    def to_side(z, p, i):
        return remote(spot(z, p), spot(z, p), sib_send.at[i], w_recv.at[z, p], (grp, side, me))

    def wait_piece(z, p):
        to_side(z, p, 0).wait_recv()

    def fan_out(z):
        turn = lax.rem(z - me + n, n) - 1
        copies = [to_side(z, plane, turn * (len(others) + 1))]
        for i, (dg, dt) in enumerate(others):
            g2, t2 = mate(dg, dt)
            copies.append(
                remote(
                    spot(z, plane), spot(z, plane), plane_send.at[turn * len(others) + i], w_recv.at[z, plane], (g2, t2, me)
                )
            )
        return copies

    def pass_on(z):
        turn = lax.rem(z - me + n, n) - 1
        found = []
        for i, (dg, dt) in enumerate(others):
            g2, t2 = mate(dg, dt)
            p = g2 * nt + t2
            found.append((p, to_side(z, p, turn * (len(others) + 1) + 1 + i)))
        return found

    def both(distance, act):
        low, high = me - distance, me + distance
        pl.when(low >= 0)(lambda: act(jnp.maximum(low, 0)))
        pl.when(high < n)(lambda: act(jnp.minimum(high, n - 1)))

    def fan(z):
        wait_piece(z, plane)
        for copy in fan_out(z)[::-1]:
            copy.start()

    def hand(z):
        for p, copy in pass_on(z):
            wait_piece(z, p)
            copy.start()

    def settle(z):
        for dg in range(ng):
            for dt in range(0, nt, 2):
                wait_piece(z, lax.rem(grp + dg, ng) * nt + lax.rem(side + dt, nt))

    chunks = width // step
    acc[...] = jnp.zeros_like(acc)

    def chunk(c, carry):
        slot = lax.rem(c, 2)

        @pl.when(c + 1 < chunks)
        def _():
            for copy in load(c + 1, 1 - slot):
                copy.start()

        for copy in load(c, slot):
            copy.wait()
        acc[...] += mm(x_buf[slot], wk_buf[slot], 1, 0)
        return carry

    half = chunks // 2
    lax.fori_loop(0, half, chunk, 0)
    for dt in range(2, nt, 2):
        t2 = lax.rem(ten + dt, nt)
        wait_adapters(t2)
        send_adapters(t2, side, dt + 1)
    both(1, fan)
    lax.fori_loop(half, chunks, chunk, 0)
    if n > 2:
        both(2, fan)
    for dt in range(0, nt, 2):
        wait_adapters(lax.rem(side + dt, nt))

    ids = lax.broadcasted_iota(jnp.int32, (stored, 1), 0) // rank
    mask = ids == want_ref[...]
    fold = (
        lax.rem(lax.broadcasted_iota(jnp.int32, (stored, rank), 0), rank)
        == lax.broadcasted_iota(jnp.int32, (stored, rank), 1)
    ).astype(BF16)
    own_x.wait()
    part = jnp.where(mask, mm(a_ref[...], x_cols[...], 1, 1), 0.0).astype(BF16)
    rank_out[:rank, :] = mm(fold, part, 0, 0).astype(BF16)
    part = jnp.where(mask, mm(b_ref[...], g_ref[...], 1, 1), 0.0).astype(BF16)
    rank_out[rank:, :] = mm(fold, part, 0, 0).astype(BF16)
    rank_sends = []
    for k in range(1, n):
        copy = remote(rank_out, rank_in.at[me], rank_send.at[k], rank_recv.at[me], at_tensor(line(k)))
        copy.start()
        rank_sends.append(copy)

    tile = min(narrow, 512)

    def add_block(o, g_block, first):
        def body(c, carry):
            cols = pl.ds(pl.multiple_of(c * tile, tile), tile)
            term = mm(g_block[...], w_buf[o, cols, :], 1, 1)
            if first:
                total[:, cols] = term
            else:
                total[:, cols] += term
            return carry

        lax.fori_loop(0, narrow // tile, body, 0)

    for d in range(3, n):
        both(d, fan)
    own_w.wait()
    add_block(me, g_ref, True)
    both(1, hand)

    rank_in[me] = rank_out[...]
    for k in range(1, n):
        z = line(k)
        remote(rank_out, rank_in.at[z], rank_send.at[k], rank_recv.at[z], at_tensor(z)).wait_recv()
    whole = rank_in[0].astype(F32)
    for z in range(1, n):
        whole = whole + rank_in[z].astype(F32)
    twice = (whole.astype(BF16).astype(F32) * 2.0).astype(BF16)
    shrink = jnp.where(mask, mm(fold, twice[:rank, :], 1, 0), 0.0).astype(BF16)
    back_ref[...] = jnp.where(mask, mm(fold, twice[rank:, :], 1, 0), 0.0).astype(BF16)

    if n > 2:
        relay(0)
    for p in range(nt):
        grad_out[p, :, :narrow] = mm(back_ref[pl.ds(p * owned, owned), :], x_cols[...], 1, 0).astype(BF16)
    spread = mm(shrink, g_ref[...], 1, 0).astype(BF16)
    for p in range(nt):
        grad_out[p, :, narrow:] = spread[p * owned : (p + 1) * owned, :]
    grad_sends = []
    for dt in range(0, nt, 2):
        t2 = lax.rem(side + dt, nt)
        copy = remote(grad_out.at[t2], grad_side.at[t2], grad_send.at[dt], side_recv.at[t2], (grp, side, me))
        copy.start()
        grad_sends.append(copy)
    kv_ref[...] = (acc[...] + mm(shrink, b_ref[...], 0, 0)).astype(BF16)

    for dt in range(0, nt, 2):
        t2 = lax.rem(ten + dt, nt)
        remote(grad_out.at[t2], grad_side.at[t2], grad_send.at[0], side_recv.at[t2], (grp, side, me)).wait_recv()
        if dt:
            grad_out[t2] = (grad_out[t2].astype(F32) + grad_side[t2].astype(F32)).astype(BF16)
            copy = remote(grad_out.at[t2], grad_in.at[ten], grad_send.at[dt + 1], grad_recv.at[ten], (grp, t2, me))
            copy.start()
            grad_sends.append(copy)

    def add_adapter(c, carry):
        cols = pl.ds(pl.multiple_of(c * tile, tile), tile)
        total[:, cols] += mm(back_ref[...], a_ref[:, cols], 0, 0)
        return carry

    lax.fori_loop(0, narrow // tile, add_adapter, 0)
    def use(s):
        low, high = me - 1 - s, me + 1 + s

        @pl.when(low >= 0)
        def _():
            o = jnp.maximum(low, 0)
            add_block(o, g_buf.at[o], False)

        @pl.when(high < n)
        def _():
            o = jnp.minimum(high, n - 1)
            add_block(o, g_buf.at[o], False)

    for d in range(2, n):
        both(d, hand)
    for s in range(n - 2):
        if s:
            relay(s)
        both(s + 1, settle)
        use(s)

    ag = grad_out[ten, :, :narrow].astype(F32) + grad_side[ten, :, :narrow].astype(F32)
    bg = grad_out[ten, :, narrow:].astype(F32) + grad_side[ten, :, narrow:].astype(F32)
    for dt in range(2, nt, 2):
        t2 = lax.rem(ten + dt, nt)
        remote(grad_out.at[t2], grad_in.at[t2], grad_send.at[0], grad_recv.at[t2], (grp, t2, me)).wait_recv()
        ag = ag + grad_in[t2, :, :narrow].astype(F32)
        bg = bg + grad_in[t2, :, narrow:].astype(F32)
    ag_ref[...] = ag
    bg_ref[...] = bg

    both(n - 1, settle)

    def finish(o):
        for c in range(parts):
            arrived(n - 2, c)
            span = pl.ds(c * part_rows, part_rows)

            def body(i, carry):
                cols = pl.ds(pl.multiple_of(i * tile, tile), tile)
                term = mm(g_buf[o, span, :], w_buf[o, cols, :], 1, 1)
                in_ref[span, cols] = (total[span, cols] + term).astype(BF16)
                return carry

            lax.fori_loop(0, narrow // tile, body, 0)

    pl.when(me == n - 1)(lambda: finish(0))
    pl.when(me == 0)(lambda: finish(n - 1))

    @pl.when(jnp.logical_and(me > 0, me < n - 1))
    def _():
        in_ref[...] = total[...].astype(BF16)

    for k in range(1, n):
        z = line(k)
        for copy in fan_out(z) + [copy for _, copy in pass_on(z)]:
            copy.wait_send()
    for copy in w_sends + rank_sends + grad_sends + adapter_sends:
        copy.wait_send()
    for s in range(n - 1):
        for c in range(parts):
            for ok, copy in (up(s, c), down(s, c)):
                pl.when(ok)(copy.wait_send)


def local(tokens, kv_weight, cotangent, a_store, b_store, tile_tenant, tenant_place):
    rows, model_width = tokens.shape
    tiles = tile_tenant.shape[0]
    tile_len = rows // tiles
    slots, rank, narrow = a_store.shape
    part_cols = kv_weight.shape[2]
    wide = 2 * part_cols
    tenants = tenant_place.shape[0]
    n = lax.axis_size("tensor")
    nt = lax.axis_size("tenant")
    ng = lax.axis_size("groups")
    piece = narrow // (ng * nt)

    stored = nt * slots * rank
    w_flat = kv_weight.reshape(model_width, wide)
    g_flat = cotangent.reshape(rows, wide)
    lookup = tile_tenant[:, None] == jnp.arange(tenants, dtype=jnp.int32)[None, :]
    wanted = jnp.sum(jnp.where(lookup, tenant_place[None, :], 0), axis=1)
    want_rows = jnp.repeat(wanted, tile_len)[None, :]

    step = 1024 if model_width % 1024 == 0 else model_width // 2
    vmem = pl.BlockSpec(memory_space=pltpu.VMEM)
    hbm = pl.BlockSpec(memory_space=pl.ANY)
    dma = pltpu.SemaphoreType.DMA
    mates = ng * nt // 2
    parts = 2
    kv, inp, ag, bg = pl.pallas_call(
        functools.partial(kernel, (n, ng, nt, piece, rank, step, parts)),
        out_shape=(
            jax.ShapeDtypeStruct((rows, wide), BF16),
            jax.ShapeDtypeStruct((rows, narrow), BF16),
            jax.ShapeDtypeStruct((slots * rank, narrow), F32),
            jax.ShapeDtypeStruct((slots * rank, wide), F32),
        ),
        in_specs=[hbm, hbm, vmem, vmem, vmem, vmem],
        out_specs=(vmem, vmem, vmem, vmem),
        scratch_shapes=[
            pltpu.VMEM((2, rows, step), BF16),
            pltpu.VMEM((2, step, wide), BF16),
            pltpu.VMEM((rows, wide), F32),
            pltpu.VMEM((rows, narrow), BF16),
            pltpu.VMEM((n, narrow, wide), BF16),
            pltpu.VMEM((n, rows, wide), BF16),
            pltpu.VMEM((rows, narrow), F32),
            pltpu.VMEM((2 * rank, rows), BF16),
            pltpu.VMEM((n, 2 * rank, rows), BF16),
            pltpu.VMEM((nt, slots * rank, narrow + wide), BF16),
            pltpu.VMEM((nt, slots * rank, narrow + wide), BF16),
            pltpu.VMEM((nt, slots * rank, narrow + wide), BF16),
            pltpu.VMEM((stored, rows), BF16),
            pltpu.VMEM((stored, narrow), BF16),
            pltpu.VMEM((stored, wide), BF16),
            dma((2,)),
            dma((2,)),
            dma((2,)),
            dma((n,)),
            dma((n, ng * nt)),
            dma(((n - 1) * max(mates - 1, 1),)),
            dma(((n - 1) * mates,)),
            dma((n * parts,)),
            dma((n * parts,)),
            dma((n * parts,)),
            dma((n * parts,)),
            dma((n,)),
            dma((n,)),
            dma((nt,)),
            dma((nt,)),
            dma((nt,)),
            dma((nt,)),
            dma((nt,)),
            dma((nt,)),
            dma((nt,)),
        ],
        compiler_params=pltpu.CompilerParams(
            collective_id=0, has_side_effects=True, vmem_limit_bytes=60 * 1024 * 1024
        ),
    )(
        tokens,
        w_flat,
        g_flat,
        a_store.reshape(slots * rank, narrow),
        b_store.reshape(slots * rank, wide),
        want_rows,
    )
    return (
        kv.reshape(rows, 2, part_cols),
        inp,
        ag.reshape(slots, rank, narrow),
        bg.reshape(slots, rank, 2, part_cols),
    )


def solution(mesh):
    in_specs = (
        P(("groups", "tenant"), None),
        P(None, None, "tensor"),
        P(("groups", "tenant"), None, "tensor"),
        P("tenant", None, "tensor"),
        P("tenant", None, None, "tensor"),
        P(("groups", "tenant")),
        P(),
    )
    out_specs = (
        P(("groups", "tenant"), None, "tensor"),
        P(("groups", "tenant"), "tensor"),
        P(("groups", "tenant"), None, "tensor"),
        P(("groups", "tenant"), None, None, "tensor"),
    )
    return jax.shard_map(local, mesh=mesh, in_specs=in_specs, out_specs=out_specs, check_vma=False)
```
